32 devices in a mesh: expert: 8 (over z, x), half: 4 (over y, core).
Axes of the slice: x: 2, y: 2, z: 4, core: 2. Of those that a mesh axis runs over, the one named last changes fastest.
Arguments:
- tokens: bfloat16 [8192, 1024], P(('expert', 'half')), may hold values from -6 to 6
- router: bfloat16 [1024, 16], replicated, may hold values from -1 to 1
- w_in: bfloat16 [8, 1024, 3072], P('expert', None, 'half'), may hold values from -0.1875 to 0.1875
- w_out: bfloat16 [8, 3072, 1024], P('expert', 'half'), may hold values from -0.109375 to 0.109375
Outputs:
- mixed: bfloat16 [8192, 1024], P(('expert', 'half'))
The draws below stay inside these ranges and needn't reach their ends.
All inputs are finite; a program needn't handle non-finite values.
Results may differ from the reference program's by a relative error of at most 0.018.
Values may be sent and summed in bfloat16 or wider, within the bound.
A program may use at most 64 MiB of HBM per device.

```python
import jax
import jax.numpy as jnp
from jax import lax

D = 1024
FF = 3072
SLOTS = 2
PATCHES = 256
EXPERTS = 8
IMAGES = 32
TOKENS = 8192
N_HALF = 4


def joint_draw(key):
    base = jax.random.fold_in(key, 7)
    key_tokens, key_router = jax.random.split(base, 2)
    columns = EXPERTS * SLOTS
    tokens = jnp.clip(jax.random.normal(key_tokens, (TOKENS, D), jnp.float32), -6.0, 6.0)
    router = jnp.clip(jax.random.normal(key_router, (D, columns), jnp.float32), -6.0, 6.0) * D ** (-0.5)
    return (tokens, router)


def draw_tokens(key, part):
    return joint_draw(key)[0].astype(jnp.bfloat16)


def draw_router(key, part):
    return joint_draw(key)[1].astype(jnp.bfloat16)


def levels(stream_key, dims, shards, least, high):
    gain, own = 1.0, jax.random.fold_in(stream_key, 6)
    for dim, shards_of in shards:
        heights = jnp.exp(jax.random.uniform(jax.random.fold_in(own, dim), (shards_of,), jnp.float32, least / len(shards), high / len(shards)))
        gain = gain * jnp.repeat(heights, dims[dim] // shards_of).reshape([-1 if axis == dim else 1 for axis in range(len(dims))])
    return gain


def noise(stream_key, dims, spread, reach, shards=(), kind=jnp.bfloat16):
    entries = jax.random.normal(stream_key, dims, jnp.float32) * spread
    if len(shards) > 0:
        entries = levels(stream_key, dims, shards, -0.22, 0.18) * entries
    return jnp.clip(entries, min=-reach, max=reach).astype(kind)


def setup_inputs(seed: int = 0) -> dict:
    seeds = jax.random.split(jax.random.key(seed), 5)
    return {
        "tokens": draw_tokens(jax.random.fold_in(seeds[4], 71), 0),
        "router": draw_router(jax.random.fold_in(seeds[4], 71), 0),
        "w_in": noise(seeds[2], (EXPERTS, D, FF), D ** -0.5, 0.1875, ((0, 8), (2, 4))),
        "w_out": noise(seeds[3], (EXPERTS, FF, D), FF ** -0.5, 0.109375, ((0, 8), (1, 4))),
    }


def expert_apply(operands):
    rows, first, second = operands
    share = FF // N_HALF
    total = jnp.zeros((rows.shape[0], D), jnp.float32)
    for quarter in range(N_HALF):
        left = first[:, quarter * share:(quarter + 1) * share].astype(jnp.float32)
        right = second[quarter * share:(quarter + 1) * share, :].astype(jnp.float32)
        hidden = jax.nn.gelu(jnp.dot(rows.astype(jnp.float32), left, precision=lax.Precision.HIGHEST)).astype(jnp.bfloat16)
        partial_out = jnp.dot(hidden.astype(jnp.float32), right, precision=lax.Precision.HIGHEST).astype(jnp.bfloat16)
        total = total + lax.optimization_barrier(partial_out).astype(jnp.float32)
    return total.astype(jnp.bfloat16)


def reference(tokens, router, w_in, w_out):
    columns = EXPERTS * SLOTS
    picture = tokens.reshape(IMAGES, PATCHES, D).astype(jnp.float32)
    logits = jnp.einsum("imd,dc->imc", picture, router.astype(jnp.float32), precision=lax.Precision.HIGHEST)
    dispatch = jax.nn.softmax(logits, axis=1).astype(jnp.bfloat16)
    combine = jax.nn.softmax(logits, axis=2).astype(jnp.bfloat16)
    slot_input = jnp.einsum("imc,imd->icd", dispatch.astype(jnp.float32), picture, precision=lax.Precision.HIGHEST).astype(jnp.bfloat16)
    per_expert = slot_input.reshape(IMAGES, EXPERTS, SLOTS, D).transpose(1, 0, 2, 3).reshape(EXPERTS, IMAGES * SLOTS, D)
    outputs = lax.map(expert_apply, (per_expert, w_in, w_out))
    slot_output = outputs.reshape(EXPERTS, IMAGES, SLOTS, D).transpose(1, 0, 2, 3).reshape(IMAGES, columns, D)
    mixed = jnp.einsum("imc,icd->imd", combine.astype(jnp.float32), slot_output.astype(jnp.float32), precision=lax.Precision.HIGHEST)
    return mixed.astype(jnp.bfloat16).reshape(TOKENS, D)
```

```python
import functools

import jax
import jax.numpy as jnp
from jax import lax
from jax.experimental import pallas as pl
from jax.experimental.pallas import tpu as pltpu
from jax.sharding import PartitionSpec as P

SLOTS = 2
LANES = 128
MESH = pl.DeviceIdType.MESH
F32 = jnp.float32
BF16 = jnp.bfloat16


def swap_matrix(blocks):
    size = blocks * blocks * SLOTS
    row = lax.broadcasted_iota(jnp.int32, (size, size), 0)
    column = lax.broadcasted_iota(jnp.int32, (size, size), 1)
    line = blocks * SLOTS
    a, b, s = row // line, (row % line) // SLOTS, row % SLOTS
    return jnp.where(column == b * line + a * SLOTS + s, 1.0, 0.0).astype(BF16)


def to_messages(swap, rows, blocks):
    line = blocks * SLOTS
    groups = rows.shape[0] // line
    stacked = [
        jnp.concatenate(
            [
                rows[g * line:(g + 1) * line, j * LANES:(j + 1) * LANES]
                for j in range(blocks)
            ],
            axis=0,
        )
        for g in range(groups)
    ]
    moved = jnp.dot(swap, jnp.concatenate(stacked, axis=1), preferred_element_type=F32).astype(BF16)
    return [
        moved[:, g * LANES:(g + 1) * LANES].reshape(blocks, line, LANES) for g in range(groups)
    ]


def to_rows(swap, tiles, blocks):
    line = blocks * SLOTS
    groups = tiles.shape[0] // blocks
    stacked = jnp.concatenate(
        [
            tiles[g * blocks:(g + 1) * blocks].reshape(blocks * line, LANES)
            for g in range(groups)
        ],
        axis=1,
    )
    moved = jnp.dot(swap, stacked, preferred_element_type=F32).astype(BF16)
    return jnp.concatenate(
        [
            jnp.concatenate(
                [
                    moved[j * line:(j + 1) * line, g * LANES:(g + 1) * LANES]
                    for j in range(blocks)
                ],
                axis=1,
            )
            for g in range(groups)
        ],
        axis=0,
    )


def kernel(
    experts, halves,
    tokens_ref, router_ref, w_in_ref, w_out_ref, out_ref,
    tok, rout, first, second, send, recv, part, ret, mixed,
    in_sems, out_sems, send_sems, recv_sems,
):
    devices = experts * halves
    me_e, me_h = lax.axis_index("expert"), lax.axis_index("half")
    me = me_e * halves + me_h
    patches, width = tok.shape
    blocks = width // LANES

    loads = [
        pltpu.make_async_copy(src, dst, in_sems.at[k])
        for k, (src, dst) in enumerate(
            [(tokens_ref, tok), (router_ref, rout), (w_in_ref.at[0], first), (w_out_ref.at[0], second)]
        )
    ]
    for load in loads:
        load.start()

    def others(act):
        for dh in range(1, halves):
            act(me_e, lax.rem(me_h + dh, halves))

        @pl.loop(1, experts)
        def _(de):
            e = lax.rem(me_e + de, experts)
            for dh in range(halves):
                act(e, lax.rem(me_h + dh, halves))

    barrier = pltpu.get_barrier_semaphore()
    others(lambda e, h: pl.semaphore_signal(barrier, inc=1, device_id=(e, h), device_id_type=MESH))

    swap = swap_matrix(blocks)

    loads[0].wait()
    loads[1].wait()
    logits = lax.dot_general(
        rout[...], tok[...], (((1,), (1,)), ((), ())), preferred_element_type=F32
    )
    up = jnp.exp(logits - jnp.max(logits, axis=1, keepdims=True))
    dispatch = (up / jnp.sum(up, axis=1, keepdims=True)).astype(BF16)
    slot_input = jnp.dot(dispatch, tok[...], preferred_element_type=F32).astype(BF16)
    for g, tiles in enumerate(to_messages(swap, slot_input, blocks)):
        send[g * blocks:(g + 1) * blocks] = tiles

    pl.semaphore_wait(barrier, devices - 1)

    def dispatch_to(e, h):
        pltpu.make_async_remote_copy(
            src_ref=send.at[e], dst_ref=recv.at[me],
            send_sem=send_sems.at[0], recv_sem=recv_sems.at[0],
            device_id=(e, h), device_id_type=MESH,
        ).start()

    others(dispatch_to)
    pltpu.make_async_copy(send.at[me_e], recv.at[me], recv_sems.at[0]).start()

    across = jnp.exp(logits - jnp.max(logits, axis=0, keepdims=True))
    combine = (across / jnp.sum(across, axis=0, keepdims=True)).astype(F32)
    combine = combine.T.astype(BF16)

    loads[2].wait()
    loads[3].wait()
    pltpu.make_async_copy(recv, recv, recv_sems.at[0]).wait()

    rows = to_rows(swap, recv[...], blocks)
    hidden = jax.nn.gelu(jnp.dot(rows, first[...], preferred_element_type=F32)).astype(BF16)
    terms = jnp.dot(hidden, second[...], preferred_element_type=F32).astype(BF16)
    for g, tiles in enumerate(to_messages(swap, terms, blocks)):
        part[g * blocks:(g + 1) * blocks] = tiles

    place = me_h * experts + me_e

    def return_to(e, h):
        pltpu.make_async_remote_copy(
            src_ref=part.at[e * halves + h], dst_ref=ret.at[place],
            send_sem=send_sems.at[1], recv_sem=recv_sems.at[1],
            device_id=(e, h), device_id_type=MESH,
        ).start()

    others(return_to)
    pltpu.make_async_copy(part.at[me], ret.at[place], recv_sems.at[1]).start()
    pltpu.make_async_copy(ret, ret, recv_sems.at[1]).wait()

    total = ret[0:experts].astype(F32)
    for h in range(1, halves):
        total = total + ret[h * experts:(h + 1) * experts].astype(F32)
    slot_output = to_rows(swap, total.astype(BF16), blocks)

    chunks = 4
    chunk = patches // chunks
    stores = []
    for k in range(chunks):
        span = pl.ds(k * chunk, chunk)
        mixed[span, :] = jnp.dot(
            combine[k * chunk:(k + 1) * chunk], slot_output, preferred_element_type=F32
        ).astype(BF16)
        store = pltpu.make_async_copy(mixed.at[span], out_ref.at[span], out_sems.at[k])
        store.start()
        stores.append(store)

    sent = recv.at[pl.ds(0, devices - 1)]
    for k in range(2):
        pltpu.make_async_copy(sent, sent, send_sems.at[k]).wait()
    for store in stores:
        store.wait()


def solution(mesh):
    experts, halves = mesh.shape["expert"], mesh.shape["half"]
    devices = experts * halves

    def on_device(tokens, router, w_in, w_out):
        patches, width = tokens.shape
        share = w_in.shape[2]
        columns = router.shape[1]
        tile = (SLOTS * width // LANES, LANES)
        dma = pltpu.SemaphoreType.DMA
        return pl.pallas_call(
            functools.partial(kernel, experts, halves),
            out_shape=jax.ShapeDtypeStruct((patches, width), BF16),
            in_specs=[pl.BlockSpec(memory_space=pl.ANY)] * 4,
            out_specs=pl.BlockSpec(memory_space=pl.ANY),
            scratch_shapes=[
                pltpu.VMEM((patches, width), BF16),
                pltpu.VMEM((columns, width), BF16),
                pltpu.VMEM((width, share), BF16),
                pltpu.VMEM((share, width), BF16),
                pltpu.VMEM((experts, *tile), BF16),
                pltpu.VMEM((devices, *tile), BF16),
                pltpu.VMEM((devices, *tile), BF16),
                pltpu.VMEM((devices, *tile), BF16),
                pltpu.VMEM((patches, width), BF16),
                dma((4,)),
                dma((4,)),
                dma((2,)),
                dma((2,)),
            ],
            compiler_params=pltpu.CompilerParams(
                collective_id=0, has_side_effects=True, vmem_limit_bytes=56 * 2**20
            ),
            name="soft_moe",
        )(tokens, router.T, w_in, w_out)

    return jax.shard_map(
        on_device,
        mesh=mesh,
        in_specs=(
            P(("expert", "half"), None),
            P(),
            P("expert", None, "half"),
            P("expert", "half", None),
        ),
        out_specs=P(("expert", "half"), None),
        check_vma=False,
    )
```

```python
import functools

import jax
import jax.numpy as jnp
from jax import lax
from jax.experimental import pallas as pl
from jax.experimental.pallas import tpu as pltpu
from jax.sharding import PartitionSpec as P

SLOTS = 2
LANES = 128
MESH = pl.DeviceIdType.MESH
F32 = jnp.float32
BF16 = jnp.bfloat16


def swap_matrix(blocks):
    size = blocks * blocks * SLOTS
    row = lax.broadcasted_iota(jnp.int32, (size, size), 0)
    column = lax.broadcasted_iota(jnp.int32, (size, size), 1)
    line = blocks * SLOTS
    a, b, s = row // line, (row % line) // SLOTS, row % SLOTS
    return jnp.where(column == b * line + a * SLOTS + s, 1.0, 0.0).astype(BF16)


def to_messages(swap, rows, blocks):
    line = blocks * SLOTS
    groups = rows.shape[0] // line
    stacked = [
        jnp.concatenate(
            [
                rows[g * line:(g + 1) * line, j * LANES:(j + 1) * LANES]
                for j in range(blocks)
            ],
            axis=0,
        )
        for g in range(groups)
    ]
    moved = jnp.dot(swap, jnp.concatenate(stacked, axis=1), preferred_element_type=F32).astype(BF16)
    return [
        moved[:, g * LANES:(g + 1) * LANES].reshape(blocks, line, LANES) for g in range(groups)
    ]


def to_rows(swap, tiles, blocks):
    line = blocks * SLOTS
    groups = tiles.shape[0] // blocks
    stacked = jnp.concatenate(
        [
            tiles[g * blocks:(g + 1) * blocks].reshape(blocks * line, LANES)
            for g in range(groups)
        ],
        axis=1,
    )
    moved = jnp.dot(swap, stacked, preferred_element_type=F32).astype(BF16)
    return jnp.concatenate(
        [
            jnp.concatenate(
                [
                    moved[j * line:(j + 1) * line, g * LANES:(g + 1) * LANES]
                    for j in range(blocks)
                ],
                axis=1,
            )
            for g in range(groups)
        ],
        axis=0,
    )


def mix_kernel(combine_ref, slots_ref, out_ref, mixed, sems):
    combine = combine_ref[...].astype(F32).T.astype(BF16)
    chunks = sems.shape[0]
    chunk = mixed.shape[0] // chunks
    stores = []
    for k in range(chunks):
        span = pl.ds(k * chunk, chunk)
        mixed[span, :] = jnp.dot(
            combine[k * chunk:(k + 1) * chunk], slots_ref[...], preferred_element_type=F32
        ).astype(BF16)
        store = pltpu.make_async_copy(mixed.at[span], out_ref.at[span], sems.at[k])
        store.start()
        stores.append(store)
    for store in stores:
        store.wait()


def exclusive_or(a, b, size):
    value, bit = 0, 1
    while bit < size:
        value = value + bit * lax.rem(lax.div(a, bit) + lax.div(b, bit), 2)
        bit *= 2
    return value


def kernel(
    experts, halves,
    tokens_ref, router_ref, w_in_ref, w_out_ref, mixed_rows, combine_out,
    tok, rout, first, second, send, recv, part, ret,
    in_sems, send_sems, recv_sems,
):
    devices = experts * halves
    me_e, me_h = lax.axis_index("expert"), lax.axis_index("half")
    me = me_e * halves + me_h
    patches, width = tok.shape
    blocks = width // LANES

    loads = [
        pltpu.make_async_copy(src, dst, in_sems.at[k])
        for k, (src, dst) in enumerate(
            [(tokens_ref, tok), (router_ref, rout), (w_in_ref.at[0], first), (w_out_ref.at[0], second)]
        )
    ]
    loads[0].start()
    loads[1].start()

    order = [exclusive_or(me_h, jnp.int32(d), halves) for d in reversed(range(halves))]

    def others(act):
        @pl.loop(1, experts)
        def _(k):
            e = exclusive_or(me_e, experts - k, experts)
            for h in order:
                act(e, h)

        for h in order[:-1]:
            act(me_e, h)

    barrier = pltpu.get_barrier_semaphore()
    others(lambda e, h: pl.semaphore_signal(barrier, inc=1, device_id=(e, h), device_id_type=MESH))
    loads[2].start()
    loads[3].start()

    swap = swap_matrix(blocks)

    loads[0].wait()
    loads[1].wait()
    logits = lax.dot_general(
        rout[...], tok[...], (((1,), (1,)), ((), ())), preferred_element_type=F32
    )
    up = jnp.exp(logits - jnp.max(logits, axis=1, keepdims=True))
    dispatch = (up / jnp.sum(up, axis=1, keepdims=True)).astype(BF16)
    slot_input = jnp.dot(dispatch, tok[...], preferred_element_type=F32).astype(BF16)
    for g, tiles in enumerate(to_messages(swap, slot_input, blocks)):
        send[g * blocks:(g + 1) * blocks] = tiles

    pl.semaphore_wait(barrier, devices - 1)

    def dispatch_to(e, h):
        pltpu.make_async_remote_copy(
            src_ref=send.at[e], dst_ref=recv.at[me],
            send_sem=send_sems.at[0], recv_sem=recv_sems.at[0],
            device_id=(e, h), device_id_type=MESH,
        ).start()

    others(dispatch_to)
    pltpu.make_async_copy(send.at[me_e], recv.at[me], recv_sems.at[0]).start()

    across = jnp.exp(logits - jnp.max(logits, axis=0, keepdims=True))
    combine_t = (across / jnp.sum(across, axis=0, keepdims=True)).astype(BF16)

    loads[2].wait()
    loads[3].wait()
    pltpu.make_async_copy(recv, recv, recv_sems.at[0]).wait()

    rows = to_rows(swap, recv[...], blocks)
    hidden = jax.nn.gelu(jnp.dot(rows, first[...], preferred_element_type=F32)).astype(BF16)
    terms = jnp.dot(hidden, second[...], preferred_element_type=F32).astype(BF16)
    for g, tiles in enumerate(to_messages(swap, terms, blocks)):
        part[g * blocks:(g + 1) * blocks] = tiles

    place = me_h * experts + me_e

    def return_to(e, h):
        pltpu.make_async_remote_copy(
            src_ref=part.at[e * halves + h], dst_ref=ret.at[place],
            send_sem=send_sems.at[1], recv_sem=recv_sems.at[1],
            device_id=(e, h), device_id_type=MESH,
        ).start()

    others(return_to)
    pltpu.make_async_copy(part.at[me], ret.at[place], recv_sems.at[1]).start()
    pltpu.make_async_copy(ret, ret, recv_sems.at[1]).wait()

    total = ret[0:experts].astype(F32)
    for h in range(1, halves):
        total = total + ret[h * experts:(h + 1) * experts].astype(F32)
    slot_output = to_rows(swap, total.astype(BF16), blocks)

    mixed_rows[...] = slot_output
    combine_out[...] = combine_t

    sent = recv.at[pl.ds(0, devices - 1)]
    for k in range(2):
        pltpu.make_async_copy(sent, sent, send_sems.at[k]).wait()


def solution(mesh):
    experts, halves = mesh.shape["expert"], mesh.shape["half"]
    devices = experts * halves

    def on_device(tokens, router, w_in, w_out):
        patches, width = tokens.shape
        share = w_in.shape[2]
        columns = router.shape[1]
        tile = (SLOTS * width // LANES, LANES)
        dma = pltpu.SemaphoreType.DMA
        slot_output, combine = pl.pallas_call(
            functools.partial(kernel, experts, halves),
            out_shape=[jax.ShapeDtypeStruct((columns, width), BF16), jax.ShapeDtypeStruct((columns, patches), BF16)],
            in_specs=[pl.BlockSpec(memory_space=pltpu.HBM)] * 4,
            out_specs=[pl.BlockSpec(memory_space=pltpu.VMEM)] * 2,
            scratch_shapes=[
                pltpu.VMEM((patches, width), BF16),
                pltpu.VMEM((columns, width), BF16),
                pltpu.VMEM((width, share), BF16),
                pltpu.VMEM((share, width), BF16),
                pltpu.VMEM((experts, *tile), BF16),
                pltpu.VMEM((devices, *tile), BF16),
                pltpu.VMEM((devices, *tile), BF16),
                pltpu.VMEM((devices, *tile), BF16),
                dma((4,)),
                dma((2,)),
                dma((2,)),
            ],
            compiler_params=pltpu.CompilerParams(
                collective_id=0, has_side_effects=True, vmem_limit_bytes=55168 * 2**10
            ),
            name="soft_moe",
        )(tokens, router.T, w_in, w_out)
        return pl.pallas_call(
            mix_kernel,
            out_shape=jax.ShapeDtypeStruct((patches, width), BF16),
            in_specs=[pl.BlockSpec(memory_space=pltpu.VMEM)] * 2,
            out_specs=pl.BlockSpec(memory_space=pl.ANY),
            scratch_shapes=[pltpu.VMEM((patches, width), BF16), dma((4,))],
            compiler_params=pltpu.CompilerParams(vmem_limit_bytes=16 * 2**20),
            name="mix",
        )(combine, slot_output)

    return jax.shard_map(
        on_device,
        mesh=mesh,
        in_specs=(
            P(("expert", "half"), None),
            P(),
            P("expert", None, "half"),
            P("expert", "half", None),
        ),
        out_specs=P(("expert", "half"), None),
        check_vma=False,
    )
```
